128 devices in a mesh: tm: 16 (over y_hi, x, core), cuts: 8 (over y_lo, z).
Axes of the slice: x: 4, y: 4 (y_hi: 2, y_lo: 2; y = y_hi * 2 + y_lo), z: 4, core: 2. Of those that a mesh axis runs over, the one named last changes fastest.
Arguments:
- volume: float32 [32, 64, 24, 1024], P('tm', 'cuts'), may hold values from -6 to 6
- measured: bfloat16 [32, 6, 64, 24, 1024], P('tm', None, 'cuts'), may hold values from -6 to 6
- counts: int32 [32], P('tm'), may hold values from 2 to 6, as said below
- vshift: int32 [32, 6], P('tm'), may hold values from -2 to 2, as said below
- hshift: int32 [32, 6], P('tm'), may hold values from -16 to 16
- angles: int32 [32, 6], P('tm'), may hold values from 0 to 3
- blocks: bfloat16 [4, 1024, 1024], replicated, may hold values from -0.1875 to 0.1875
Outputs:
- gradient: float32 [32, 64, 24, 1024], P('tm', 'cuts')
The draws below stay inside these ranges and needn't reach their ends.
Inputs may be any that keep to these rules, and one draw needn't show every extreme that they name: `counts`: some frame has exactly 2 live views and another exactly 6. `vshift`: some live view has the shift 2 and another -2.
All inputs are finite; a program needn't handle non-finite values.
Results may differ from the reference program's by a relative error of at most 0.0029.
Values may be sent and summed in bfloat16 or wider, within the bound.
No kernel may reach another device: no remote copies, remote signals or barrier semaphores. Data moves between devices by JAX's collectives and lax.ppermute only.
A program may use at most 64 MiB of HBM per device.

```python
from functools import partial
import jax
import jax.numpy as jnp
from jax import lax

Y = 1024
DET = 1024
XW = 24
VCAP = 6
NA = 4
H = 2
SH = 16
F = 32
Z = 64


def draw_counts(key, part):
    values = jax.random.randint(key, (F,), 2, VCAP + 1)
    picked = jax.random.fold_in(key, 21)
    frame_low = jax.random.randint(jax.random.fold_in(picked, 1), (), 0, F)
    frame_high = (frame_low + 1 + jax.random.randint(jax.random.fold_in(picked, 2), (), 0, F - 1)) % F
    values = values.at[frame_low].set(2).at[frame_high].set(VCAP)
    return values.astype(jnp.int32)


def draw_vshift(key, part):
    values = jax.random.randint(key, (F, VCAP), -H, H + 1)
    picked = jax.random.fold_in(key, 37)
    frame_low = jax.random.randint(jax.random.fold_in(picked, 1), (), 0, F)
    frame_high = jax.random.randint(jax.random.fold_in(picked, 2), (), 0, F)
    view_low = jax.random.randint(jax.random.fold_in(picked, 3), (), 0, 1)
    view_high = 1 - view_low
    values = values.at[frame_low, view_low].set(-H).at[frame_high, view_high].set(H)
    return values.astype(jnp.int32)


def place_ends(array, key, least, top_value):
    dims = array.shape
    index_at = [jax.random.randint(jax.random.fold_in(key, axis), (), 0, dims[axis]) for axis in range(len(dims))]
    array = array.at[tuple(index_at)].set(least)
    longest = dims.index(max(dims))
    index_at[longest] = (index_at[longest] + 1) % dims[longest]
    return array.at[tuple(index_at)].set(top_value)


def level_of(rng, dims, cuts, least, high):
    gain, own = 1.0, jax.random.fold_in(rng, 6)
    for dim, shards_of in cuts:
        steps = jnp.exp(jax.random.uniform(jax.random.fold_in(own, dim), (shards_of,), jnp.float32, least / len(cuts), high / len(cuts)))
        gain = gain * jnp.repeat(steps, dims[dim] // shards_of).reshape([-1 if axis == dim else 1 for axis in range(len(dims))])
    return gain


def scatter_about(stream_key, dims, width, reach, shards=(), held_as=jnp.bfloat16):
    drawn = jax.random.normal(stream_key, dims, jnp.float32) * width
    if len(shards) > 0:
        drawn = level_of(stream_key, dims, shards, -0.22, 0.18) * drawn
    return jnp.clip(drawn, min=-reach, max=reach).astype(held_as)


def setup_inputs(seed: int = 0) -> dict:
    arg_keys = jax.random.split(jax.random.key(seed), 8)
    volume = scatter_about(arg_keys[0], (F, Z, XW, Y), 1.0, 6.0, ((0, 16), (1, 8)), jnp.float32)
    measured = scatter_about(arg_keys[1], (F, VCAP, Z, XW, DET), 1.0, 6.0, ((0, 16), (2, 8)))
    counts = draw_counts(jax.random.fold_in(arg_keys[7], 71), 0)
    vshift = draw_vshift(jax.random.fold_in(arg_keys[7], 71), 0)
    hshift = place_ends(jax.random.randint(arg_keys[4], (F, VCAP), -SH, SH + 1), jax.random.fold_in(arg_keys[4], 1), -SH, SH).astype(jnp.int32)
    angles = place_ends(jax.random.randint(arg_keys[5], (F, VCAP), 0, NA), jax.random.fold_in(arg_keys[5], 1), 0, NA - 1).astype(jnp.int32)
    blocks = scatter_about(arg_keys[6], (NA, Y, DET), Y ** -0.5, 0.1875)
    return {"volume": volume, "measured": measured, "counts": counts, "vshift": vshift, "hshift": hshift, "angles": angles, "blocks": blocks}


def shift_cols(values, amount):
    padded = jnp.pad(values, [(0, 0)] * (values.ndim - 1) + [(SH, SH)])
    return lax.dynamic_slice_in_dim(padded, SH - amount, values.shape[-1], values.ndim - 1)

def view_residual(extended, measured_frame, vertical, lateral, angle_ids, blocks, count, masked, view_no, totals):
    slices = measured_frame.shape[1]
    block = lax.dynamic_index_in_dim(blocks, angle_ids[view_no], 0, keepdims=False)
    offset = H + vertical[view_no]
    lateral_now = lateral[view_no]
    source_frame = lax.dynamic_slice_in_dim(extended, offset, slices, 0)
    image = jnp.dot(source_frame.reshape(-1, source_frame.shape[-1]), block, preferred_element_type=jnp.float32)
    image = image.reshape(measured_frame.shape[1:])
    seen = lax.dynamic_index_in_dim(measured_frame, view_no, 0, keepdims=False)
    misfit = shift_cols(image, lateral_now) - seen.astype(jnp.float32)
    if masked:
        misfit = misfit * (view_no < count).astype(jnp.float32)
    spread = shift_cols(misfit.astype(jnp.bfloat16), -lateral_now)
    back = lax.dot_general(spread.reshape(-1, spread.shape[-1]), block, (((1,), (1,)), ((), ())), preferred_element_type=jnp.float32)
    back = back.reshape(source_frame.shape)
    present_frame = lax.dynamic_slice_in_dim(totals, offset, slices, 0)
    return lax.dynamic_update_slice_in_dim(totals, present_frame + back, offset, 0)

def reference(volume, measured, counts, vshift, hshift, angles, blocks):
    lowered = volume.astype(jnp.bfloat16)
    extended = jnp.pad(lowered, ((0, 0), (H, H), (0, 0), (0, 0)))

    def frame_fit(frame_number):
        extended_frame_index = lax.dynamic_index_in_dim(extended, frame_number, 0, keepdims=False)
        measurement_frame = lax.dynamic_index_in_dim(measured, frame_number, 0, keepdims=False)
        step_forward = partial(view_residual, extended_frame_index, measurement_frame, vshift[frame_number], hshift[frame_number], angles[frame_number], blocks, counts[frame_number], True)
        totals = lax.fori_loop(0, VCAP, step_forward, jnp.zeros(extended_frame_index.shape, jnp.float32))
        return totals[H:H + Z]
    fitted_volume = lax.map(frame_fit, jnp.arange(F, dtype=jnp.int32))
    differ = volume[1:] - volume[:-1]
    weight = differ / jnp.sqrt(differ * differ + 0.25)
    varied = jnp.pad(weight, ((1, 0), (0, 0), (0, 0), (0, 0))) - jnp.pad(weight, ((0, 1), (0, 0), (0, 0), (0, 0)))
    return fitted_volume + 0.5 * varied
```

```python
import jax
import jax.numpy as jnp
from jax import lax
from jax.experimental import pallas as pl
from jax.experimental.pallas import tpu as pltpu
from jax.sharding import PartitionSpec as P

H = 2
NA = 4
LANES = 128
BF16 = jnp.bfloat16
F32 = jnp.float32
NT = (((1,), (1,)), ((), ()))


def lateral(buf, index, h, width):
    start = pl.multiple_of(jnp.where(h < 0, 0, LANES), LANES)
    part = h & (LANES - 1)
    amount = (LANES - part) & (LANES - 1)
    values = buf[index + (slice(None), pl.ds(start, width + LANES))].astype(F32)
    tiles = width // LANES
    turned = [
        pltpu.roll(values[:, j * LANES : (j + 1) * LANES], amount, 1) for j in range(tiles + 1)
    ]
    lane = lax.broadcasted_iota(jnp.int32, turned[0].shape, 1)
    near = lane < LANES - part
    return jnp.concatenate(
        [jnp.where(near, turned[j], turned[j + 1]) for j in range(tiles)], axis=1
    )


def rim_kernel(
    counts, vshift, hshift, angles, measured, blocks, volume,
    up, down, first, last, edge, table, vol, sums, total, edge_sem, block_sem, vol_sem,
):
    frames, views, slices, rows, width = measured.shape
    inner = pl.ds(LANES, width)
    low_copy = pltpu.make_async_copy(
        measured.at[:, :, 0:H], edge.at[:, :, 0:H, :, inner], edge_sem.at[0])
    high_copy = pltpu.make_async_copy(
        measured.at[:, :, slices - H : slices], edge.at[:, :, H : 2 * H, :, inner], edge_sem.at[1])
    vol_copy = pltpu.make_async_copy(volume, vol, vol_sem)
    block_copies = [
        pltpu.make_async_copy(blocks.at[a], table.at[a], block_sem.at[a]) for a in range(NA)
    ]
    low_copy.start()
    high_copy.start()
    for copy in block_copies:
        copy.start()
    vol_copy.start()
    pad = jnp.zeros((frames, views, 2 * H, rows, LANES), BF16)
    edge[:, :, :, :, 0:LANES] = pad
    edge[:, :, :, :, width + LANES : width + 2 * LANES] = pad
    sums[...] = jnp.zeros_like(sums)
    low_copy.wait()
    high_copy.wait()

    def add_view(i, carry):
        f = i // views
        v = i - f * views
        s = vshift[f, v]
        h = hshift[f, v]
        a = angles[f, v]
        parts = jnp.where(v < counts[f], jnp.abs(s), 0)

        def add_slice(k, carry):
            source = jnp.where(s > 0, 2 * H - s + k, k)
            slot = jnp.where(s > 0, H + k, k + s + H)
            sums[a, f * 2 * H + slot] += lateral(edge, (f, v, source), h, width)
            return carry

        return lax.fori_loop(0, parts, add_slice, carry)

    lax.fori_loop(0, frames * views, add_view, 0)
    for a in range(NA):
        block_copies[a].wait()
        part = (-sums[a]).reshape(frames * 2 * H * rows, width).astype(BF16)
        back = lax.dot_general(part, table[a], NT, preferred_element_type=F32)
        if a == 0:
            total[...] = back
        else:
            total[...] += back
    vol_copy.wait()
    first[...] = vol[0:1].astype(BF16)
    last[...] = vol[1:2].astype(BF16)
    rims = total[...].reshape(frames, 2 * H, rows, width).astype(BF16)
    down[...] = rims[:, 0:H]
    up[...] = rims[:, H : 2 * H]


def fit_kernel(
    counts, vshift, hshift, angles, measured, blocks, volume,
    fit, meas, table, vol, image, sums, live, meas_sem, block_sem, vol_sem,
):
    frames, views, slices, rows, width = measured.shape
    inner = pl.ds(LANES, width)
    n = frames * slices * rows
    vol_copy = pltpu.make_async_copy(volume, vol, vol_sem)
    block_copies = [
        pltpu.make_async_copy(blocks.at[a], table.at[a], block_sem.at[a]) for a in range(NA)
    ]
    meas_copies = [
        pltpu.make_async_copy(measured.at[f, v], meas.at[f, v, :, :, inner], meas_sem.at[f, v])
        for f in range(frames) for v in range(views)
    ]
    vol_copy.start()
    block_copies[0].start()
    per = frames * views // NA
    for a in range(NA):
        for copy in meas_copies[a * per : (a + 1) * per]:
            copy.start()
        if a + 1 < NA:
            block_copies[a + 1].start()
    pad = jnp.zeros((frames, views, slices, rows, LANES), BF16)
    meas[:, :, :, :, 0:LANES] = pad
    meas[:, :, :, :, width + LANES : width + 2 * LANES] = pad
    sums[...] = jnp.zeros_like(sums)
    live[...] = jnp.zeros_like(live)
    here = lax.axis_index("cuts")
    end = lax.axis_size("cuts") * slices
    place = lax.broadcasted_iota(jnp.int32, (slices, width), 0) + here * slices
    lane = lax.broadcasted_iota(jnp.int32, (slices, width), 1)
    vol_copy.wait()
    low = vol[...].reshape(n, width).astype(BF16)
    for a in range(NA):
        block_copies[a].wait()
        for copy in meas_copies[a * per : (a + 1) * per]:
            copy.wait()
        image[a] = jnp.dot(low, table[a], preferred_element_type=F32)
        for i in range(a * per, (a + 1) * per):
            f, v = divmod(i, views)
            s = vshift[f, v]
            h = hshift[f, v]
            slot = jnp.where(v < counts[f], angles[f, v], NA)
            seen = (lane + h >= 0) & (lane + h < width) & (place - s >= 0) & (place - s < end)
            live[f, slot] += jnp.where(seen, 1.0, 0.0)
            for z in range(slices):
                sums[f, slot, H + s + z] += lateral(meas, (f, v, z), h, width)
    for a in range(NA):
        parts = []
        for f in range(frames):
            for z in range(slices):
                at = (f * slices + z) * rows
                scale = live[f, a, z : z + 1, :]
                parts.append(image[a, at : at + rows] * scale - sums[f, a, H + z])
        misfit = jnp.concatenate(parts, axis=0).astype(BF16)
        back = lax.dot_general(misfit, table[a], NT, preferred_element_type=F32)
        back = back.reshape(frames, slices, rows, width)
        if a == 0:
            fit[...] = back
        else:
            fit[...] += back


def weight(differ):
    return differ / jnp.sqrt(differ * differ + 0.25)


def join_kernel(fit, volume, before, after, below, above, out):
    frames, slices = fit.shape[0], fit.shape[1]
    t, c = lax.axis_index("tm"), lax.axis_index("cuts")
    has_before = jnp.where(t > 0, 0.5, 0.0)
    has_after = jnp.where(t < lax.axis_size("tm") - 1, 0.5, 0.0)
    has_below = jnp.where(c > 0, 1.0, 0.0)
    has_above = jnp.where(c < lax.axis_size("cuts") - 1, 1.0, 0.0)
    for z in range(slices):
        edge = [before[0, z].astype(F32)] + [volume[f, z] for f in range(frames)]
        edge.append(after[0, z].astype(F32))
        factor = [has_before] + [0.5] * (frames - 1) + [has_after]
        w = [weight(edge[k + 1] - edge[k]) * factor[k] for k in range(frames + 1)]
        for f in range(frames):
            value = fit[f, z] + (w[f] - w[f + 1])
            if z < H:
                value += below[f, z].astype(F32) * has_below
            if z >= slices - H:
                value += above[f, z - slices + H].astype(F32) * has_above
            out[f, z] = value


def ring(x, axis, by):
    size = lax.axis_size(axis)
    return lax.ppermute(x, axis, [(i, (i + by) % size) for i in range(size)])


def body(volume, measured, counts, vshift, hshift, angles, blocks):
    frames, views, slices, rows, width = measured.shape
    smem = pl.BlockSpec(memory_space=pltpu.SMEM)
    anyw = pl.BlockSpec(memory_space=pl.ANY)
    vmem = pl.BlockSpec(memory_space=pltpu.VMEM)
    shape = jax.ShapeDtypeStruct
    wide = width + 2 * LANES
    dma = pltpu.SemaphoreType.DMA
    up, down, first, last = pl.pallas_call(
        rim_kernel,
        out_shape=[
            shape((frames, H, rows, width), BF16),
            shape((frames, H, rows, width), BF16),
            shape((1, slices, rows, width), BF16),
            shape((1, slices, rows, width), BF16),
        ],
        in_specs=[smem] * 4 + [anyw] * 3,
        out_specs=[vmem] * 4,
        scratch_shapes=[
            pltpu.VMEM((frames, views, 2 * H, rows, wide), BF16),
            pltpu.VMEM(blocks.shape, BF16),
            pltpu.VMEM(volume.shape, F32),
            pltpu.VMEM((NA, frames * 2 * H, rows, width), F32),
            pltpu.VMEM((frames * 2 * H * rows, width), F32),
            dma((2,)),
            dma((NA,)),
            dma,
        ],
        compiler_params=pltpu.CompilerParams(vmem_limit_bytes=48 * 2**20),
        cost_estimate=pl.CostEstimate(
            flops=2 * NA * frames * 2 * H * rows * width * width, bytes_accessed=14 * 2**20,
            transcendentals=0),
        name="rims",
    )(counts, vshift, hshift, angles, measured, blocks, volume)
    below = ring(up, "cuts", 1)
    above = ring(down, "cuts", -1)
    before = ring(last, "tm", 1)
    after = ring(first, "tm", -1)
    fit = pl.pallas_call(
        fit_kernel,
        out_shape=shape(volume.shape, F32),
        in_specs=[smem] * 4 + [anyw] * 3,
        out_specs=vmem,
        scratch_shapes=[
            pltpu.VMEM((frames, views, slices, rows, wide), BF16),
            pltpu.VMEM(blocks.shape, BF16),
            pltpu.VMEM(volume.shape, F32),
            pltpu.VMEM((NA, frames * slices * rows, width), F32),
            pltpu.VMEM((frames, NA + 1, slices + 2 * H, rows, width), F32),
            pltpu.VMEM((frames, NA + 1, slices, width), F32),
            dma((frames, views)),
            dma((NA,)),
            dma,
        ],
        compiler_params=pltpu.CompilerParams(vmem_limit_bytes=60 * 2**20),
        cost_estimate=pl.CostEstimate(
            flops=4 * NA * frames * slices * rows * width * width, bytes_accessed=16 * 2**20,
            transcendentals=0),
        name="fit",
    )(counts, vshift, hshift, angles, measured, blocks, volume)
    return pl.pallas_call(
        join_kernel,
        out_shape=shape(volume.shape, F32),
        in_specs=[vmem] * 6,
        out_specs=vmem,
        compiler_params=pltpu.CompilerParams(vmem_limit_bytes=32 * 2**20),
        name="join",
    )(fit, volume, before, after, below, above)


def solution(mesh):
    in_specs = (
        P("tm", "cuts", None, None),
        P("tm", None, "cuts", None, None),
        P("tm"),
        P("tm", None),
        P("tm", None),
        P("tm", None),
        P(),
    )
    out_specs = P("tm", "cuts", None, None)
    return jax.shard_map(body, mesh=mesh, in_specs=in_specs, out_specs=out_specs, check_vma=False)
```

```python
import jax
import jax.numpy as jnp
from jax import lax
from jax.experimental import pallas as pl
from jax.experimental.pallas import tpu as pltpu
from jax.sharding import PartitionSpec as P

H = 2
NA = 4
CHUNKS = 4
LANES = 128
BF16 = jnp.bfloat16
F32 = jnp.float32
NT = (((1,), (1,)), ((), ()))


def lateral(buf, index, h, width):
    start = pl.multiple_of(jnp.where(h < 0, 0, LANES), LANES)
    part = h & (LANES - 1)
    amount = (LANES - part) & (LANES - 1)
    values = buf[index + (slice(None), pl.ds(start, width + LANES))].astype(F32)
    tiles = width // LANES
    turned = [
        pltpu.roll(values[:, j * LANES : (j + 1) * LANES], amount, 1) for j in range(tiles + 1)
    ]
    lane = lax.broadcasted_iota(jnp.int32, turned[0].shape, 1)
    near = lane < LANES - part
    return jnp.concatenate(
        [jnp.where(near, turned[j], turned[j + 1]) for j in range(tiles)], axis=1
    )


def weight(differ):
    return differ * lax.rsqrt(differ * differ + 0.25)


def rim_kernel(
    counts_in, vshift_in, hshift_in, angles_in, measured, blocks, volume,
    up, down, first, last, table, meas, low, vol,
    counts, vshift, hshift, angles, sums, part, total,
    int_sem, meas_sem, block_sem, vol_sem,
):
    frames, views, slices, rows, width = measured.shape
    inner = pl.ds(LANES, width)
    int_copies = [
        pltpu.make_async_copy(a, b, int_sem.at[i])
        for i, (a, b) in enumerate(
            [(counts_in, counts), (vshift_in, vshift), (hshift_in, hshift), (angles_in, angles)])
    ]
    cuts = [(0, H), (slices - H, H), (H, slices - 2 * H)]
    meas_copies = [
        pltpu.make_async_copy(
            measured.at[:, :, z : z + k], meas.at[:, :, z : z + k, :, inner], meas_sem.at[i])
        for i, (z, k) in enumerate(cuts)
    ]
    vol_copy = pltpu.make_async_copy(volume, vol, vol_sem)
    block_copies = [
        pltpu.make_async_copy(blocks.at[a], table.at[a], block_sem.at[a]) for a in range(NA)
    ]
    for copy in int_copies + meas_copies[:2] + block_copies + [vol_copy] + meas_copies[2:]:
        copy.start()
    pad = jnp.zeros((slices, rows, LANES), BF16)
    for f in range(frames):
        for v in range(views):
            meas[f, v, :, :, 0:LANES] = pad
            meas[f, v, :, :, width + LANES : width + 2 * LANES] = pad
    edge = frames * 2 * H * rows
    spare = jnp.zeros((part.shape[1] - edge, width), BF16)
    nothing = jnp.zeros((rows, width), F32)
    for a in range(NA):
        part[a, edge:] = spare
        for k in range(frames * 2 * H):
            sums[a, k] = nothing
    for copy in int_copies + meas_copies[:2]:
        copy.wait()
    for f in range(frames):
        for v in range(views):
            s = vshift[f, v]
            h = hshift[f, v]
            for k in range(H):
                used = (v < counts[f]) & (k < jnp.abs(s))
                a = jnp.where(used, angles[f, v], NA)
                source = jnp.where(used & (s > 0), slices - s + k, k)
                slot = jnp.where(used, jnp.where(s > 0, H + k, H + k + s), 0)
                sums[a, f * 2 * H + slot] += lateral(meas, (f, v, source), h, width)
    pair = 2 * rows
    for a in range(NA):
        for k in range(frames * H):
            part[a, k * pair : (k + 1) * pair] = (
                sums[a, 2 * k : 2 * k + 2].reshape(pair, width).astype(BF16))
    for a in range(NA):
        block_copies[a].wait()
        for c in range(CHUNKS):
            at = slice(c * width // CHUNKS, (c + 1) * width // CHUNKS)
            back = lax.dot_general(table[a, at], part[a], NT, preferred_element_type=F32)
            if a == 0:
                total[at] = back
            else:
                total[at] += back
    vol_copy.wait()
    for f in range(frames):
        for z in range(0, slices, 2):
            at = (f * slices + z) * rows
            low[at : at + pair] = vol[f, z : z + 2].reshape(pair, width).astype(BF16)
    first[...] = vol[0:1].astype(BF16)
    last[...] = vol[frames - 1 : frames].astype(BF16)
    turned = -(total[...].T)
    for f in range(frames):
        at = f * 2 * pair
        down[f] = turned[at : at + pair].reshape(H, rows, width).astype(BF16)
        up[f] = turned[at + pair : at + 2 * pair].reshape(H, rows, width).astype(BF16)
    for copy in meas_copies[2:]:
        copy.wait()


def fit_kernel(
    counts_in, vshift_in, hshift_in, angles_in, meas, table, low, vol,
    fit, counts, vshift, hshift, angles, image, sums, live, misfit, middle, int_sem,
):
    frames, views, slices, rows, wide = meas.shape
    width = wide - 2 * LANES
    int_copies = [
        pltpu.make_async_copy(a, b, int_sem.at[i])
        for i, (a, b) in enumerate(
            [(counts_in, counts), (vshift_in, vshift), (hshift_in, hshift), (angles_in, angles)])
    ]
    for copy in int_copies:
        copy.start()
    nothing = jnp.zeros((rows, width), F32)
    chunk = width // CHUNKS

    def clear(f, a):
        live[f, a] = jnp.zeros((slices, width), F32)
        for z in range(slices):
            sums[f, a, H + z] = nothing

    def add_slice(f, v, z):
        slot = jnp.where(v < counts[f], angles[f, v], NA)
        sums[f, slot, H + vshift[f, v] + z] += lateral(meas, (f, v, z), hshift[f, v], width)

    def add_live(f, v):
        here = lax.axis_index("cuts")
        end = lax.axis_size("cuts") * slices
        place = lax.broadcasted_iota(jnp.int32, (slices, width), 0) + here * slices - vshift[f, v]
        lane = lax.broadcasted_iota(jnp.int32, (slices, width), 1) + hshift[f, v]
        seen = (lane >= 0) & (lane < width) & (place >= 0) & (place < end)
        slot = jnp.where(v < counts[f], angles[f, v], NA)
        live[f, slot] += jnp.where(seen, 1.0, 0.0)

    def make_misfit(a, f, z):
        at = (f * slices + z) * rows
        both = [
            image[a, at + k * rows : at + (k + 1) * rows] * live[f, a, z + k : z + k + 1, :]
            - sums[f, a, H + z + k]
            for k in range(2)
        ]
        misfit[a, at : at + 2 * rows] = jnp.concatenate(both, axis=0).astype(BF16)

    def forward(a, c):
        image[a, :, c * chunk : (c + 1) * chunk] = jnp.dot(
            low[...], table[a, :, c * chunk : (c + 1) * chunk], preferred_element_type=F32)

    def backward(a, c):
        at = slice(c * chunk, (c + 1) * chunk)
        back = lax.dot_general(misfit[a], table[a, at], NT, preferred_element_type=F32)
        if a == 0:
            half = n // frames
            fit[0:half, at] = back[0:half] - middle[:, at]
            fit[half:n, at] = back[half:n] + middle[:, at]
        else:
            fit[:, at] += back

    def add_middle(z):
        middle[z * rows : (z + 1) * rows] = weight(vol[1, z] - vol[0, z]) * 0.5

    n = frames * slices * rows
    clears = [(f, a) for f in range(frames) for a in range(NA)]
    adds = [(f, v, z) for f in range(frames) for v in range(views) for z in range(slices)]
    steps = [(a, c) for a in range(NA) for c in range(CHUNKS)]
    lead = CHUNKS
    for i, step in enumerate(steps):
        forward(*step)
        if i < lead:
            for item in clears[i * len(clears) // lead : (i + 1) * len(clears) // lead]:
                clear(*item)
            for z in range(i * slices // lead, (i + 1) * slices // lead):
                add_middle(z)
        else:
            if i == lead:
                for copy in int_copies:
                    copy.wait()
            k, m = i - lead, len(steps) - lead
            for item in adds[k * len(adds) // m : (k + 1) * len(adds) // m]:
                add_slice(*item)
                if item[2] == 0:
                    add_live(*item[:2])
    pairs = [(f, z) for f in range(frames) for z in range(0, slices, 2)]
    for item in pairs:
        make_misfit(0, *item)
    for a in range(NA):
        for c in range(CHUNKS):
            backward(a, c)
            if a + 1 < NA:
                for item in pairs[c * len(pairs) // CHUNKS : (c + 1) * len(pairs) // CHUNKS]:
                    make_misfit(a + 1, *item)


def join_kernel(fit, volume, before, after, below, above, out, held, sem):
    frames, slices, rows, width = volume.shape
    t, c = lax.axis_index("tm"), lax.axis_index("cuts")
    has_before = jnp.where(t > 0, 0.5, 0.0)
    has_after = jnp.where(t < lax.axis_size("tm") - 1, 0.5, 0.0)
    has_below = jnp.where(c > 0, 1.0, 0.0)
    has_above = jnp.where(c < lax.axis_size("cuts") - 1, 1.0, 0.0)
    copies = []
    for z in range(slices):
        start = weight(volume[0, z] - before[0, z].astype(F32)) * has_before
        stop = weight(after[0, z].astype(F32) - volume[1, z]) * has_after
        for f in range(frames):
            at = (f * slices + z) * rows
            value = fit[at : at + rows] + (start if f == 0 else -stop)
            if z < H:
                value += below[f, z].astype(F32) * has_below
            if z >= slices - H:
                value += above[f, z - slices + H].astype(F32) * has_above
            held[f, z] = value
        copies.append(pltpu.make_async_copy(held.at[:, z], out.at[:, z], sem.at[z]))
        copies[-1].start()
    for copy in copies:
        copy.wait()


def ring(x, axis, by):
    size = lax.axis_size(axis)
    return lax.ppermute(x, axis, [(i, (i + by) % size) for i in range(size)])


def body(volume, measured, counts, vshift, hshift, angles, blocks):
    frames, views, slices, rows, width = measured.shape
    hbm = pl.BlockSpec(memory_space=pltpu.HBM)
    held = pltpu.with_memory_space_constraint
    vmem = pl.BlockSpec(memory_space=pltpu.VMEM)
    shape = jax.ShapeDtypeStruct
    wide = width + 2 * LANES
    dma = pltpu.SemaphoreType.DMA
    n = frames * slices * rows
    edge = pl.cdiv(frames * 2 * H * rows, LANES) * LANES
    ints = [held(x, pltpu.HBM) for x in (counts, vshift, hshift, angles)]
    int_scratch = [pltpu.SMEM(x.shape, jnp.int32) for x in ints]
    up, down, first, last, table, meas, low, vol = pl.pallas_call(
        rim_kernel,
        out_shape=[
            pltpu.VMEM((frames, H, rows, width), BF16),
            pltpu.VMEM((frames, H, rows, width), BF16),
            pltpu.VMEM((1, slices, rows, width), BF16),
            pltpu.VMEM((1, slices, rows, width), BF16),
            pltpu.VMEM(blocks.shape, BF16),
            pltpu.VMEM((frames, views, slices, rows, wide), BF16),
            pltpu.VMEM((n, width), BF16),
            pltpu.VMEM(volume.shape, F32),
        ],
        in_specs=[hbm] * 7,
        out_specs=[vmem] * 8,
        scratch_shapes=int_scratch + [
            pltpu.VMEM((NA + 1, frames * 2 * H, rows, width), F32),
            pltpu.VMEM((NA, edge, width), BF16),
            pltpu.VMEM((width, edge), F32),
            dma((4,)),
            dma((3,)),
            dma((NA,)),
            dma,
        ],
        compiler_params=pltpu.CompilerParams(vmem_limit_bytes=14 * 2**20),
        cost_estimate=pl.CostEstimate(
            flops=2 * NA * edge * width * width, bytes_accessed=16 * 2**20, transcendentals=0),
        name="rims",
    )(*ints, *(held(x, pltpu.HBM) for x in (measured, blocks, volume)))
    below = ring(up, "cuts", 1)
    above = ring(down, "cuts", -1)
    before = ring(last, "tm", 1)
    after = ring(first, "tm", -1)
    fit = pl.pallas_call(
        fit_kernel,
        out_shape=pltpu.VMEM((n, width), F32),
        in_specs=[hbm] * 4 + [vmem] * 4,
        out_specs=vmem,
        scratch_shapes=int_scratch + [
            pltpu.VMEM((NA, n, width), F32),
            pltpu.VMEM((frames, NA + 1, slices + 2 * H, rows, width), F32),
            pltpu.VMEM((frames, NA + 1, slices, width), F32),
            pltpu.VMEM((NA, n, width), BF16),
            pltpu.VMEM((slices * rows, width), F32),
            dma((4,)),
        ],
        compiler_params=pltpu.CompilerParams(vmem_limit_bytes=30 * 2**20),
        cost_estimate=pl.CostEstimate(
            flops=4 * NA * n * width * width, bytes_accessed=16 * 2**20, transcendentals=0),
        name="fit",
    )(*ints, *(held(x, pltpu.VMEM) for x in (meas, table, low, vol)))
    return pl.pallas_call(
        join_kernel,
        out_shape=shape(volume.shape, F32),
        in_specs=[vmem] * 6,
        out_specs=hbm,
        scratch_shapes=[pltpu.VMEM(volume.shape, F32), dma((slices,))],
        compiler_params=pltpu.CompilerParams(vmem_limit_bytes=8 * 2**20),
        name="join",
    )(*(held(x, pltpu.VMEM) for x in (fit, vol, before, after, below, above)))


def solution(mesh):
    in_specs = (
        P("tm", "cuts", None, None),
        P("tm", None, "cuts", None, None),
        P("tm"),
        P("tm", None),
        P("tm", None),
        P("tm", None),
        P(),
    )
    out_specs = P("tm", "cuts", None, None)
    return jax.shard_map(body, mesh=mesh, in_specs=in_specs, out_specs=out_specs, check_vma=False)
```

```python
import jax
import jax.numpy as jnp
from jax import lax
from jax.experimental import pallas as pl
from jax.experimental.pallas import tpu as pltpu
from jax.sharding import PartitionSpec as P

H = 2
NA = 4
CHUNKS = 4
LANES = 128
BF16 = jnp.bfloat16
F32 = jnp.float32
NT = (((1,), (1,)), ((), ()))


def lateral(buf, index, h, width):
    start = pl.multiple_of(jnp.where(h < 0, 0, LANES), LANES)
    part = h & (LANES - 1)
    amount = (LANES - part) & (LANES - 1)
    values = buf[index + (slice(None), pl.ds(start, width + LANES))].astype(F32)
    tiles = width // LANES
    turned = [
        pltpu.roll(values[:, j * LANES : (j + 1) * LANES], amount, 1) for j in range(tiles + 1)
    ]
    lane = lax.broadcasted_iota(jnp.int32, turned[0].shape, 1)
    near = lane < LANES - part
    return jnp.concatenate(
        [jnp.where(near, turned[j], turned[j + 1]) for j in range(tiles)], axis=1
    )


def weight(differ):
    return differ * lax.rsqrt(differ * differ + 0.25)


def rim_kernel(
    counts_in, vshift_in, hshift_in, angles_in, measured, blocks, volume,
    up, down, first, last, table, meas, low, vol,
    counts, vshift, hshift, angles, sums, part, total,
    int_sem, meas_sem, block_sem, vol_sem,
):
    frames, views, slices, rows, width = measured.shape
    inner = pl.ds(LANES, width)
    int_copies = [
        pltpu.make_async_copy(a, b, int_sem.at[i])
        for i, (a, b) in enumerate(
            [(counts_in, counts), (vshift_in, vshift), (hshift_in, hshift), (angles_in, angles)])
    ]
    cuts = [(0, H), (slices - H, H), (H, slices - 2 * H)]
    meas_copies = [
        pltpu.make_async_copy(
            measured.at[:, :, z : z + k], meas.at[:, :, z : z + k, :, inner], meas_sem.at[i])
        for i, (z, k) in enumerate(cuts)
    ]
    vol_copy = pltpu.make_async_copy(volume, vol, vol_sem)
    block_copies = [
        pltpu.make_async_copy(blocks.at[a], table.at[a], block_sem.at[a]) for a in range(NA)
    ]
    for copy in int_copies + meas_copies[:2] + block_copies + [vol_copy] + meas_copies[2:]:
        copy.start()
    pad = jnp.zeros((slices, rows, LANES), BF16)
    for f in range(frames):
        for v in range(views):
            meas[f, v, :, :, 0:LANES] = pad
            meas[f, v, :, :, width + LANES : width + 2 * LANES] = pad
    edge = frames * 2 * H * rows
    spare = jnp.zeros((part.shape[1] - edge, width), BF16)
    nothing = jnp.zeros((rows, width), F32)
    for a in range(NA):
        part[a, edge:] = spare
        for k in range(frames * 2 * H):
            sums[a, k] = nothing
    for copy in int_copies + meas_copies[:2]:
        copy.wait()
    for f in range(frames):
        for v in range(views):
            s = vshift[f, v]
            h = hshift[f, v]
            for k in range(H):
                used = (v < counts[f]) & (k < jnp.abs(s))
                a = jnp.where(used, angles[f, v], NA)
                source = jnp.where(used & (s > 0), slices - s + k, k)
                slot = jnp.where(used, jnp.where(s > 0, H + k, H + k + s), 0)
                sums[a, f * 2 * H + slot] += lateral(meas, (f, v, source), h, width)
    pair = 2 * rows
    for a in range(NA):
        for k in range(frames * H):
            part[a, k * pair : (k + 1) * pair] = (
                sums[a, 2 * k : 2 * k + 2].reshape(pair, width).astype(BF16))
    for a in range(NA):
        block_copies[a].wait()
        for c in range(CHUNKS):
            at = slice(c * width // CHUNKS, (c + 1) * width // CHUNKS)
            back = lax.dot_general(table[a, at], part[a], NT, preferred_element_type=F32)
            if a == 0:
                total[at] = back
            else:
                total[at] += back
    vol_copy.wait()
    for f in range(frames):
        for z in range(0, slices, 2):
            at = (f * slices + z) * rows
            low[at : at + pair] = vol[f, z : z + 2].reshape(pair, width).astype(BF16)
    even = lax.axis_index("tm") % 2 == 0
    first[...] = vol[pl.ds(jnp.where(even, 0, frames - 1), 1)].astype(BF16)
    last[...] = vol[pl.ds(jnp.where(even, frames - 1, 0), 1)].astype(BF16)
    turned = -(total[...].T)
    for f in range(frames):
        at = f * 2 * pair
        down[f] = turned[at : at + pair].reshape(H, rows, width).astype(BF16)
        up[f] = turned[at + pair : at + 2 * pair].reshape(H, rows, width).astype(BF16)
    for copy in meas_copies[2:]:
        copy.wait()


def fit_kernel(
    counts_in, vshift_in, hshift_in, angles_in, meas, table, low, vol,
    fit, counts, vshift, hshift, angles, image, sums, live, misfit, middle, int_sem,
):
    frames, views, slices, rows, wide = meas.shape
    width = wide - 2 * LANES
    int_copies = [
        pltpu.make_async_copy(a, b, int_sem.at[i])
        for i, (a, b) in enumerate(
            [(counts_in, counts), (vshift_in, vshift), (hshift_in, hshift), (angles_in, angles)])
    ]
    for copy in int_copies:
        copy.start()
    nothing = jnp.zeros((rows, width), F32)
    chunk = width // CHUNKS

    def clear(f, a):
        live[f, a] = jnp.zeros((slices, width), F32)
        for z in range(slices):
            sums[f, a, H + z] = nothing

    def add_slice(f, v, z):
        slot = jnp.where(v < counts[f], angles[f, v], NA)
        sums[f, slot, H + vshift[f, v] + z] += lateral(meas, (f, v, z), hshift[f, v], width)

    def add_live(f, v):
        here = lax.axis_index("cuts")
        end = lax.axis_size("cuts") * slices
        place = lax.broadcasted_iota(jnp.int32, (slices, width), 0) + here * slices - vshift[f, v]
        lane = lax.broadcasted_iota(jnp.int32, (slices, width), 1) + hshift[f, v]
        seen = (lane >= 0) & (lane < width) & (place >= 0) & (place < end)
        slot = jnp.where(v < counts[f], angles[f, v], NA)
        live[f, slot] += jnp.where(seen, 1.0, 0.0)

    def make_misfit(a, f, z):
        at = (f * slices + z) * rows
        both = [
            image[a, at + k * rows : at + (k + 1) * rows] * live[f, a, z + k : z + k + 1, :]
            - sums[f, a, H + z + k]
            for k in range(2)
        ]
        misfit[a, at : at + 2 * rows] = jnp.concatenate(both, axis=0).astype(BF16)

    def forward(a, c):
        image[a, :, c * chunk : (c + 1) * chunk] = jnp.dot(
            low[...], table[a, :, c * chunk : (c + 1) * chunk], preferred_element_type=F32)

    def backward(a, c):
        at = slice(c * chunk, (c + 1) * chunk)
        back = lax.dot_general(misfit[a], table[a, at], NT, preferred_element_type=F32)
        if a == 0:
            half = n // frames
            fit[0:half, at] = back[0:half] - middle[:, at]
            fit[half:n, at] = back[half:n] + middle[:, at]
        else:
            fit[:, at] += back

    def add_middle(z):
        middle[z * rows : (z + 1) * rows] = weight(vol[1, z] - vol[0, z]) * 0.5

    n = frames * slices * rows
    clears = [(f, a) for f in range(frames) for a in range(NA)]
    adds = [(f, v, z) for f in range(frames) for v in range(views) for z in range(slices)]
    steps = [(a, c) for a in range(NA) for c in range(CHUNKS)]
    lead = CHUNKS
    for i, step in enumerate(steps):
        forward(*step)
        if i < lead:
            for item in clears[i * len(clears) // lead : (i + 1) * len(clears) // lead]:
                clear(*item)
            for z in range(i * slices // lead, (i + 1) * slices // lead):
                add_middle(z)
        else:
            if i == lead:
                for copy in int_copies:
                    copy.wait()
            k, m = i - lead, len(steps) - lead
            for item in adds[k * len(adds) // m : (k + 1) * len(adds) // m]:
                add_slice(*item)
                if item[2] == 0:
                    add_live(*item[:2])
    pairs = [(f, z) for f in range(frames) for z in range(0, slices, 2)]
    for item in pairs:
        make_misfit(0, *item)
    for a in range(NA):
        for c in range(CHUNKS):
            backward(a, c)
            if a + 1 < NA:
                for item in pairs[c * len(pairs) // CHUNKS : (c + 1) * len(pairs) // CHUNKS]:
                    make_misfit(a + 1, *item)


def join_kernel(fit, volume, near, far, below, above, out, held, sem):
    frames, slices, rows, width = volume.shape
    t, c = lax.axis_index("tm"), lax.axis_index("cuts")
    even = t % 2 == 0
    has_before = jnp.where(t > 0, 0.5, 0.0)
    has_after = jnp.where(t < lax.axis_size("tm") - 1, 0.5, 0.0)
    has_below = jnp.where(c > 0, 1.0, 0.0)
    has_above = jnp.where(c < lax.axis_size("cuts") - 1, 1.0, 0.0)
    copies = []
    for z in range(slices):
        close, away = near[0, z].astype(F32), far[0, z].astype(F32)
        before = jnp.where(even, away, close)
        after = jnp.where(even, close, away)
        start = weight(volume[0, z] - before) * has_before
        stop = weight(after - volume[1, z]) * has_after
        for f in range(frames):
            at = (f * slices + z) * rows
            value = fit[at : at + rows] + (start if f == 0 else -stop)
            if z < H:
                value += below[f, z].astype(F32) * has_below
            if z >= slices - H:
                value += above[f, z - slices + H].astype(F32) * has_above
            held[f, z] = value
        copies.append(pltpu.make_async_copy(held.at[:, z], out.at[:, z], sem.at[z]))
        copies[-1].start()
    for copy in copies:
        copy.wait()


def swap(x, axis, odd):
    size = lax.axis_size(axis)
    pairs = {i: i for i in range(size)}
    for i in range(odd, size - 1, 2):
        pairs[i], pairs[i + 1] = i + 1, i
    return lax.ppermute(x, axis, sorted(pairs.items()))


def ring(x, axis, by):
    size = lax.axis_size(axis)
    return lax.ppermute(x, axis, [(i, (i + by) % size) for i in range(size)])


def body(volume, measured, counts, vshift, hshift, angles, blocks):
    frames, views, slices, rows, width = measured.shape
    hbm = pl.BlockSpec(memory_space=pltpu.HBM)
    held = pltpu.with_memory_space_constraint
    vmem = pl.BlockSpec(memory_space=pltpu.VMEM)
    shape = jax.ShapeDtypeStruct
    wide = width + 2 * LANES
    dma = pltpu.SemaphoreType.DMA
    n = frames * slices * rows
    edge = pl.cdiv(frames * 2 * H * rows, LANES) * LANES
    ints = [held(x, pltpu.HBM) for x in (counts, vshift, hshift, angles)]
    int_scratch = [pltpu.SMEM(x.shape, jnp.int32) for x in ints]
    up, down, first, last, table, meas, low, vol = pl.pallas_call(
        rim_kernel,
        out_shape=[
            pltpu.VMEM((frames, H, rows, width), BF16),
            pltpu.VMEM((frames, H, rows, width), BF16),
            pltpu.VMEM((1, slices, rows, width), BF16),
            pltpu.VMEM((1, slices, rows, width), BF16),
            pltpu.VMEM(blocks.shape, BF16),
            pltpu.VMEM((frames, views, slices, rows, wide), BF16),
            pltpu.VMEM((n, width), BF16),
            pltpu.VMEM(volume.shape, F32),
        ],
        in_specs=[hbm] * 7,
        out_specs=[vmem] * 8,
        scratch_shapes=int_scratch + [
            pltpu.VMEM((NA + 1, frames * 2 * H, rows, width), F32),
            pltpu.VMEM((NA, edge, width), BF16),
            pltpu.VMEM((width, edge), F32),
            dma((4,)),
            dma((3,)),
            dma((NA,)),
            dma,
        ],
        compiler_params=pltpu.CompilerParams(vmem_limit_bytes=14 * 2**20),
        cost_estimate=pl.CostEstimate(
            flops=2 * NA * edge * width * width, bytes_accessed=16 * 2**20, transcendentals=0),
        name="rims",
    )(*ints, *(held(x, pltpu.HBM) for x in (measured, blocks, volume)))
    below = ring(up, "cuts", 1)
    above = ring(down, "cuts", -1)
    near = swap(last, "tm", 0)
    far = swap(first, "tm", 1)
    fit = pl.pallas_call(
        fit_kernel,
        out_shape=pltpu.VMEM((n, width), F32),
        in_specs=[hbm] * 4 + [vmem] * 4,
        out_specs=vmem,
        scratch_shapes=int_scratch + [
            pltpu.VMEM((NA, n, width), F32),
            pltpu.VMEM((frames, NA + 1, slices + 2 * H, rows, width), F32),
            pltpu.VMEM((frames, NA + 1, slices, width), F32),
            pltpu.VMEM((NA, n, width), BF16),
            pltpu.VMEM((slices * rows, width), F32),
            dma((4,)),
        ],
        compiler_params=pltpu.CompilerParams(vmem_limit_bytes=30 * 2**20),
        cost_estimate=pl.CostEstimate(
            flops=4 * NA * n * width * width, bytes_accessed=16 * 2**20, transcendentals=0),
        name="fit",
    )(*ints, *(held(x, pltpu.VMEM) for x in (meas, table, low, vol)))
    return pl.pallas_call(
        join_kernel,
        out_shape=shape(volume.shape, F32),
        in_specs=[vmem] * 6,
        out_specs=hbm,
        scratch_shapes=[pltpu.VMEM(volume.shape, F32), dma((slices,))],
        compiler_params=pltpu.CompilerParams(vmem_limit_bytes=8 * 2**20),
        name="join",
    )(*(held(x, pltpu.VMEM) for x in (fit, vol, near, far, below, above)))


def solution(mesh):
    in_specs = (
        P("tm", "cuts", None, None),
        P("tm", None, "cuts", None, None),
        P("tm"),
        P("tm", None),
        P("tm", None),
        P("tm", None),
        P(),
    )
    out_specs = P("tm", "cuts", None, None)
    return jax.shard_map(body, mesh=mesh, in_specs=in_specs, out_specs=out_specs, check_vma=False)
```

```python
import jax
import jax.numpy as jnp
from jax import lax
from jax.experimental import pallas as pl
from jax.experimental.pallas import tpu as pltpu
from jax.sharding import PartitionSpec as P

H = 2
NA = 4
CHUNKS = 4
LANES = 128
BF16 = jnp.bfloat16
F32 = jnp.float32
NT = (((1,), (1,)), ((), ()))


def lateral(buf, index, h, width):
    start = pl.multiple_of(jnp.where(h < 0, 0, LANES), LANES)
    part = h & (LANES - 1)
    amount = (LANES - part) & (LANES - 1)
    values = buf[index + (slice(None), pl.ds(start, width + LANES))].astype(F32)
    tiles = width // LANES
    turned = [
        pltpu.roll(values[:, j * LANES : (j + 1) * LANES], amount, 1) for j in range(tiles + 1)
    ]
    lane = lax.broadcasted_iota(jnp.int32, turned[0].shape, 1)
    near = lane < LANES - part
    return jnp.concatenate(
        [jnp.where(near, turned[j], turned[j + 1]) for j in range(tiles)], axis=1
    )


def weight(differ):
    return differ * lax.rsqrt(differ * differ + 0.25)


def rim_kernel(
    counts_in, vshift_in, hshift_in, angles_in, measured, blocks, volume,
    up, down, first, last, table, meas, low, vol,
    counts, vshift, hshift, angles, sums, part, total,
    int_sem, meas_sem, block_sem, vol_sem,
):
    frames, views, slices, rows, width = measured.shape
    inner = pl.ds(LANES, width)
    int_copies = [
        pltpu.make_async_copy(a, b, int_sem.at[i])
        for i, (a, b) in enumerate(
            [(counts_in, counts), (vshift_in, vshift), (hshift_in, hshift), (angles_in, angles)])
    ]
    cuts = [(0, H), (slices - H, H), (H, slices - 2 * H)]
    meas_copies = [
        pltpu.make_async_copy(
            measured.at[:, :, z : z + k], meas.at[:, :, z : z + k, :, inner], meas_sem.at[i])
        for i, (z, k) in enumerate(cuts)
    ]
    vol_copy = pltpu.make_async_copy(volume, vol, vol_sem)
    block_copies = [
        pltpu.make_async_copy(blocks.at[a], table.at[a], block_sem.at[a]) for a in range(NA)
    ]
    for copy in int_copies + meas_copies[:2] + block_copies + [vol_copy] + meas_copies[2:]:
        copy.start()
    pad = jnp.zeros((slices, rows, LANES), BF16)
    for f in range(frames):
        for v in range(views):
            meas[f, v, :, :, 0:LANES] = pad
            meas[f, v, :, :, width + LANES : width + 2 * LANES] = pad
    edge = frames * 2 * H * rows
    spare = jnp.zeros((part.shape[1] - edge, width), BF16)
    nothing = jnp.zeros((rows, width), F32)
    for a in range(NA):
        part[a, edge:] = spare
        for k in range(frames * 2 * H):
            sums[a, k] = nothing
    for copy in int_copies + meas_copies[:2]:
        copy.wait()
    for f in range(frames):
        for v in range(views):
            s = vshift[f, v]
            h = hshift[f, v]
            for k in range(H):
                used = (v < counts[f]) & (k < jnp.abs(s))
                a = jnp.where(used, angles[f, v], NA)
                source = jnp.where(used & (s > 0), slices - s + k, k)
                slot = jnp.where(used, jnp.where(s > 0, H + k, H + k + s), 0)
                sums[a, f * 2 * H + slot] += lateral(meas, (f, v, source), h, width)
    pair = 2 * rows
    for a in range(NA):
        for k in range(frames * H):
            part[a, k * pair : (k + 1) * pair] = (
                sums[a, 2 * k : 2 * k + 2].reshape(pair, width).astype(BF16))
    for a in range(NA):
        block_copies[a].wait()
        for c in range(CHUNKS):
            at = slice(c * width // CHUNKS, (c + 1) * width // CHUNKS)
            back = lax.dot_general(table[a, at], part[a], NT, preferred_element_type=F32)
            if a == 0:
                total[at] = back
            else:
                total[at] += back
    vol_copy.wait()
    for f in range(frames):
        for z in range(0, slices, 2):
            at = (f * slices + z) * rows
            low[at : at + pair] = vol[f, z : z + 2].reshape(pair, width).astype(BF16)
    even = lax.axis_index("tm") % 2 == 0
    first[...] = vol[pl.ds(jnp.where(even, 0, frames - 1), 1)].astype(BF16)
    last[...] = vol[pl.ds(jnp.where(even, frames - 1, 0), 1)].astype(BF16)
    turned = -(total[...].T)
    for f in range(frames):
        at = f * 2 * pair
        down[f] = turned[at : at + pair].reshape(H, rows, width).astype(BF16)
        up[f] = turned[at + pair : at + 2 * pair].reshape(H, rows, width).astype(BF16)
    for copy in meas_copies[2:]:
        copy.wait()


def fit_kernel(
    counts_in, vshift_in, hshift_in, angles_in, meas, table, low, vol,
    fit, counts, vshift, hshift, angles, image, sums, live, misfit, middle, int_sem,
):
    frames, views, slices, rows, wide = meas.shape
    width = wide - 2 * LANES
    int_copies = [
        pltpu.make_async_copy(a, b, int_sem.at[i])
        for i, (a, b) in enumerate(
            [(counts_in, counts), (vshift_in, vshift), (hshift_in, hshift), (angles_in, angles)])
    ]
    for copy in int_copies:
        copy.start()
    nothing = jnp.zeros((rows, width), F32)
    chunk = width // CHUNKS

    def clear(f, a):
        live[f, a] = jnp.zeros((slices, width), F32)
        for z in range(slices):
            sums[f, a, H + z] = nothing

    def add_slice(f, v, z):
        slot = jnp.where(v < counts[f], angles[f, v], NA)
        sums[f, slot, H + vshift[f, v] + z] += lateral(meas, (f, v, z), hshift[f, v], width)

    def add_live(f, v):
        here = lax.axis_index("cuts")
        end = lax.axis_size("cuts") * slices
        place = lax.broadcasted_iota(jnp.int32, (slices, width), 0) + here * slices - vshift[f, v]
        lane = lax.broadcasted_iota(jnp.int32, (slices, width), 1) + hshift[f, v]
        seen = (lane >= 0) & (lane < width) & (place >= 0) & (place < end)
        slot = jnp.where(v < counts[f], angles[f, v], NA)
        live[f, slot] += jnp.where(seen, 1.0, 0.0)

    def make_misfit(a, f, z):
        at = (f * slices + z) * rows
        both = [
            image[a, at + k * rows : at + (k + 1) * rows] * live[f, a, z + k : z + k + 1, :]
            - sums[f, a, H + z + k]
            for k in range(2)
        ]
        misfit[a, at : at + 2 * rows] = jnp.concatenate(both, axis=0).astype(BF16)

    def forward(a, c):
        image[a, :, c * chunk : (c + 1) * chunk] = jnp.dot(
            low[...], table[a, :, c * chunk : (c + 1) * chunk], preferred_element_type=F32)

    def backward(a, c):
        at = slice(c * chunk, (c + 1) * chunk)
        back = lax.dot_general(misfit[a], table[a, at], NT, preferred_element_type=F32)
        if a == 0:
            half = n // frames
            fit[0:half, at] = back[0:half] - middle[:, at]
            fit[half:n, at] = back[half:n] + middle[:, at]
        else:
            fit[:, at] += back

    def add_middle(z):
        middle[z * rows : (z + 1) * rows] = weight(vol[1, z] - vol[0, z]) * 0.5

    n = frames * slices * rows
    clears = [(f, a) for f in range(frames) for a in range(NA)]
    adds = [(f, v, z) for f in range(frames) for v in range(views) for z in range(slices)]
    pairs = [(f, z) for f in range(frames) for z in range(0, slices, 2)]
    steps = [(a, c) for a in range(NA) for c in range(CHUNKS)]
    lead = CHUNKS
    for i, step in enumerate(steps):
        forward(*step)
        if i < lead:
            for item in clears[i * len(clears) // lead : (i + 1) * len(clears) // lead]:
                clear(*item)
            for z in range(i * slices // lead, (i + 1) * slices // lead):
                add_middle(z)
        else:
            if i == lead:
                for copy in int_copies:
                    copy.wait()
            k, m = i - lead, len(steps) - lead - 2
            for item in adds[k * len(adds) // m : (k + 1) * len(adds) // m]:
                add_slice(*item)
                if item[2] == 0:
                    add_live(*item[:2])
            for item in pairs[max(k - m, 0) * len(pairs) // 2 : max(k - m + 1, 0) * len(pairs) // 2]:
                make_misfit(0, *item)
    for a in range(NA):
        for c in range(CHUNKS):
            backward(a, c)
            if a + 1 < NA:
                for item in pairs[c * len(pairs) // CHUNKS : (c + 1) * len(pairs) // CHUNKS]:
                    make_misfit(a + 1, *item)


def join_kernel(fit, volume, near, far, below, above, out, held, sem):
    frames, slices, rows, width = volume.shape
    t, c = lax.axis_index("tm"), lax.axis_index("cuts")
    even = t % 2 == 0
    has_before = jnp.where(t > 0, 0.5, 0.0)
    has_after = jnp.where(t < lax.axis_size("tm") - 1, 0.5, 0.0)
    has_below = jnp.where(c > 0, 1.0, 0.0)
    has_above = jnp.where(c < lax.axis_size("cuts") - 1, 1.0, 0.0)
    copies = []
    for z in range(slices):
        close, away = near[0, z].astype(F32), far[0, z].astype(F32)
        before = jnp.where(even, away, close)
        after = jnp.where(even, close, away)
        start = weight(volume[0, z] - before) * has_before
        stop = weight(after - volume[1, z]) * has_after
        for f in range(frames):
            at = (f * slices + z) * rows
            value = fit[at : at + rows] + (start if f == 0 else -stop)
            if z < H:
                value += below[f, z].astype(F32) * has_below
            if z >= slices - H:
                value += above[f, z - slices + H].astype(F32) * has_above
            held[f, z] = value
        copies.append(pltpu.make_async_copy(held.at[:, z], out.at[:, z], sem.at[z]))
        copies[-1].start()
    for copy in copies:
        copy.wait()


def swap(x, axis, odd):
    size = lax.axis_size(axis)
    pairs = {i: i for i in range(size)}
    for i in range(odd, size - 1, 2):
        pairs[i], pairs[i + 1] = i + 1, i
    return lax.ppermute(x, axis, sorted(pairs.items()))


def ring(x, axis, by):
    size = lax.axis_size(axis)
    return lax.ppermute(x, axis, [(i, (i + by) % size) for i in range(size)])


def body(volume, measured, counts, vshift, hshift, angles, blocks):
    frames, views, slices, rows, width = measured.shape
    hbm = pl.BlockSpec(memory_space=pltpu.HBM)
    held = pltpu.with_memory_space_constraint
    vmem = pl.BlockSpec(memory_space=pltpu.VMEM)
    shape = jax.ShapeDtypeStruct
    wide = width + 2 * LANES
    dma = pltpu.SemaphoreType.DMA
    n = frames * slices * rows
    edge = pl.cdiv(frames * 2 * H * rows, LANES) * LANES
    ints = [held(x, pltpu.HBM) for x in (counts, vshift, hshift, angles)]
    int_scratch = [pltpu.SMEM(x.shape, jnp.int32) for x in ints]
    up, down, first, last, table, meas, low, vol = pl.pallas_call(
        rim_kernel,
        out_shape=[
            pltpu.VMEM((frames, H, rows, width), BF16),
            pltpu.VMEM((frames, H, rows, width), BF16),
            pltpu.VMEM((1, slices, rows, width), BF16),
            pltpu.VMEM((1, slices, rows, width), BF16),
            pltpu.VMEM(blocks.shape, BF16),
            pltpu.VMEM((frames, views, slices, rows, wide), BF16),
            pltpu.VMEM((n, width), BF16),
            pltpu.VMEM(volume.shape, F32),
        ],
        in_specs=[hbm] * 7,
        out_specs=[vmem] * 8,
        scratch_shapes=int_scratch + [
            pltpu.VMEM((NA + 1, frames * 2 * H, rows, width), F32),
            pltpu.VMEM((NA, edge, width), BF16),
            pltpu.VMEM((width, edge), F32),
            dma((4,)),
            dma((3,)),
            dma((NA,)),
            dma,
        ],
        compiler_params=pltpu.CompilerParams(vmem_limit_bytes=14 * 2**20),
        cost_estimate=pl.CostEstimate(
            flops=2 * NA * edge * width * width, bytes_accessed=16 * 2**20, transcendentals=0),
        name="rims",
    )(*ints, *(held(x, pltpu.HBM) for x in (measured, blocks, volume)))
    below = ring(up, "cuts", 1)
    above = ring(down, "cuts", -1)
    near = swap(last, "tm", 0)
    far = swap(first, "tm", 1)
    fit = pl.pallas_call(
        fit_kernel,
        out_shape=pltpu.VMEM((n, width), F32),
        in_specs=[hbm] * 4 + [vmem] * 4,
        out_specs=vmem,
        scratch_shapes=int_scratch + [
            pltpu.VMEM((NA, n, width), F32),
            pltpu.VMEM((frames, NA + 1, slices + 2 * H, rows, width), F32),
            pltpu.VMEM((frames, NA + 1, slices, width), F32),
            pltpu.VMEM((NA, n, width), BF16),
            pltpu.VMEM((slices * rows, width), F32),
            dma((4,)),
        ],
        compiler_params=pltpu.CompilerParams(vmem_limit_bytes=30 * 2**20),
        cost_estimate=pl.CostEstimate(
            flops=4 * NA * n * width * width, bytes_accessed=16 * 2**20, transcendentals=0),
        name="fit",
    )(*ints, *(held(x, pltpu.VMEM) for x in (meas, table, low, vol)))
    return pl.pallas_call(
        join_kernel,
        out_shape=shape(volume.shape, F32),
        in_specs=[vmem] * 6,
        out_specs=hbm,
        scratch_shapes=[pltpu.VMEM(volume.shape, F32), dma((slices,))],
        compiler_params=pltpu.CompilerParams(vmem_limit_bytes=8 * 2**20),
        name="join",
    )(*(held(x, pltpu.VMEM) for x in (fit, vol, near, far, below, above)))


def solution(mesh):
    in_specs = (
        P("tm", "cuts", None, None),
        P("tm", None, "cuts", None, None),
        P("tm"),
        P("tm", None),
        P("tm", None),
        P("tm", None),
        P(),
    )
    out_specs = P("tm", "cuts", None, None)
    return jax.shard_map(body, mesh=mesh, in_specs=in_specs, out_specs=out_specs, check_vma=False)
```
